256 devices in a mesh: blk: 32 (over z, x_lo, core), hd: 8 (over x_hi, y).
Axes of the slice: x: 4 (x_hi: 2, x_lo: 2; x = x_hi * 2 + x_lo), y: 4, z: 8, core: 2. Of those that a mesh axis runs over, the one named last changes fastest.
Arguments:
- queries: bfloat16 [16384, 4096], P(('blk', 'hd')), may hold values from -8 to 8
- keys: bfloat16 [16384, 1024], P(('blk', 'hd')), may hold values from -8 to 8
- values: bfloat16 [16384, 1024], P(('blk', 'hd')), may hold values from -6 to 6
Outputs:
- attended: bfloat16 [16384, 4096], P(('blk', 'hd'))
The draws below stay inside these ranges and needn't reach their ends.
All inputs are finite; a program needn't handle non-finite values.
Results may differ from the reference program's by a relative error of at most 0.0044.
Values may be sent and summed in bfloat16 or wider, within the bound.
No kernel may reach another device: no remote copies, remote signals or barrier semaphores. Data moves between devices by JAX's collectives and lax.ppermute only.
A program may use at most 64 MiB of HBM per device.

```python
import jax
import jax.numpy as jnp
from jax import lax

H = 32
KV = 8
HD = 128
BLK = 256
SEQ = 16384


def base_field(key, width):
    return jnp.clip(jax.random.normal(key, (SEQ, width), jnp.float32), -6.0, 6.0)


def draw_queries(key, part):
    field = base_field(jax.random.fold_in(key, 11), H * HD)
    return field.astype(jnp.bfloat16)


def draw_keys(key, part):
    field = base_field(jax.random.fold_in(key, 12), KV * HD)
    return field.astype(jnp.bfloat16)


def block_levels(stream_key, shape, shards, low, top_value):
    level, own = 1.0, jax.random.fold_in(stream_key, 6)
    for position, blocks in shards:
        heights = jnp.exp(jax.random.uniform(jax.random.fold_in(own, position), (blocks,), jnp.float32, low / len(shards), top_value / len(shards)))
        level = level * jnp.repeat(heights, shape[position] // blocks).reshape([-1 if axis == position else 1 for axis in range(len(shape))])
    return level


def normal_values(own_key, extent, scale, most, cuts=(), kind=jnp.bfloat16):
    values = jax.random.normal(own_key, extent, jnp.float32) * scale
    if len(cuts) > 0:
        values = block_levels(own_key, extent, cuts, -0.22, 0.18) * values
    return jnp.clip(values, min=-most, max=most).astype(kind)


def setup_inputs(seed: int = 0) -> dict:
    arg_keys = jax.random.split(jax.random.key(seed), 4)
    return {
        "queries": draw_queries(jax.random.fold_in(arg_keys[3], 71), 0),
        "keys": draw_keys(jax.random.fold_in(arg_keys[3], 71), 0),
        "values": normal_values(arg_keys[2], (SEQ, KV * HD), 1.0, 6.0, ((0, 256),)),
    }


def attend_block(query_block, key_block, value_block, anchor_keys, anchor_values, has_anchor):
    group_size = H // KV
    keys_all = jnp.concatenate([anchor_keys, key_block], axis=0).astype(jnp.float32)
    values_all = jnp.concatenate([anchor_values, value_block], axis=0).astype(jnp.float32)
    keys_all = jnp.repeat(keys_all, group_size, axis=1)
    values_all = jnp.repeat(values_all, group_size, axis=1)
    scores = jnp.einsum("qhd,khd->hqk", query_block.astype(jnp.float32), keys_all) * (HD ** -0.5)
    positions = jnp.arange(BLK)[:, None]
    columns = jnp.arange(2 * BLK)[None, :]
    visible = jnp.where(columns < BLK, has_anchor, columns - BLK <= positions)
    masked = jnp.where(visible[None], scores, -jnp.inf)
    largest = jnp.max(masked, axis=-1, keepdims=True)
    raised = jnp.exp(masked - largest)
    totals = jnp.sum(raised, axis=-1, keepdims=True)
    weights = raised.astype(jnp.bfloat16)
    mixture = jnp.einsum("hqk,khd->qhd", weights.astype(jnp.float32), values_all)
    mixture = mixture / jnp.transpose(totals, (1, 0, 2))
    return mixture.astype(jnp.bfloat16)


def reference(queries, keys, values):
    block_count = SEQ // BLK
    query_blocks = queries.reshape(block_count, BLK, H, HD)
    key_blocks = keys.reshape(block_count, BLK, KV, HD)
    value_blocks = values.reshape(block_count, BLK, KV, HD)

    def attend_one(inputs):
        query_block, key_block, value_block, block_index = inputs
        return attend_block(query_block, key_block, value_block, key_blocks[0], value_blocks[0], block_index > 0)

    attended = lax.map(attend_one, (query_blocks, key_blocks, value_blocks, jnp.arange(block_count, dtype=jnp.int32)))
    return attended.reshape(SEQ, H * HD)
```

```python
import functools

import jax
import jax.numpy as jnp
import numpy as np
from jax import lax
from jax.experimental import pallas as pl
from jax.experimental.pallas import tpu as pltpu
from jax.sharding import PartitionSpec as P

H = 32
KV = 8
HD = 128
BLK = 256
ROWS = 64
GROUP = H // KV
HALF = KV // 2
RATE = HD ** (-0.5) * 1.4426950408889634
AXES = ("blk", "hd")


def place(x, y, z, core):
    return (z * 4 + (x % 2) * 2 + core) * 8 + (x // 2) * 4 + y


def whereabouts():
    blk, hd = lax.axis_index("blk"), lax.axis_index("hd")
    return (hd >> 2) * 2 + ((blk >> 1) & 1), hd & 3, blk >> 2, blk & 1


def on_chips(chips):
    x, _, z, _ = whereabouts()
    bits = 0
    for a, b in chips:
        bits |= 1 << (a * 8 + b)
    shift = (x * 8 + z).astype(jnp.uint32)
    return ((jnp.uint32(np.uint32(bits)) >> shift) & 1) == 1


def along_y(array, step, wrap):
    pairs = [
        (place(x, y, z, core), place(x, (y + step) % 4, z, core))
        for x in range(4)
        for y in range(4)
        for z in range(8)
        for core in range(2)
        if wrap or y + step < 4
    ]
    return lax.ppermute(array, AXES, pairs)


LEVELS = (((1, 0), (3, 0), (2, 0)), ((0, 2), (0, 6), (0, 4)), ((0, 1),))


def spread(piece, beside):
    have = [(0, 0)]
    for number, level in enumerate(LEVELS):
        came = []
        for dx, dz in level:
            moves = [((x, z), ((x + dx) % 4, (z + dz) % 8)) for x, z in have]
            pairs = [
                (place(a[0], y, a[1], core), place(b[0], y, b[1], core))
                for a, b in moves
                for y in range(4)
                for core in range(2)
            ]
            came.append((lax.ppermute(piece, AXES, pairs), [b for _, b in moves]))
        if number == len(LEVELS) - 1:
            (got, chips), = came
            got, beside = lax.optimization_barrier((got, beside))
            came = [(got, chips)]
        for got, chips in came:
            piece = jnp.where(on_chips(chips), got, piece)
            have = have + chips
    return piece, beside


def stacked_queries(q_ref, g):
    return jnp.concatenate(
        [q_ref[:, (g * GROUP + i) * HD : (g * GROUP + i + 1) * HD] for i in range(GROUP)], axis=0
    )


def raw_scores(query, key):
    return lax.dot_general(query, key, (((1,), (1,)), ((), ())), preferred_element_type=jnp.float32)


def own_kernel(q_ref, own_ref, one_ref, two_ref, three_ref, mix_ref, stat_ref):
    y = lax.axis_index("hd") & 3
    rows = GROUP * ROWS
    row = lax.broadcasted_iota(jnp.int32, (rows, BLK), 0) & (ROWS - 1)
    column = lax.broadcasted_iota(jnp.int32, (rows, BLK), 1)
    visible = column <= jnp.where(column < ROWS, row, y * ROWS + ROWS - 1)
    refs = (own_ref, one_ref, two_ref, three_ref)
    for g in range(KV):
        base = (g // HALF) * 2 * HALF * HD + (g % HALF) * HD
        key = jnp.concatenate([r[:, base : base + HD] for r in refs], axis=0)
        value = jnp.concatenate(
            [r[:, base + HALF * HD : base + HALF * HD + HD] for r in refs], axis=0
        )
        masked = jnp.where(visible, raw_scores(stacked_queries(q_ref, g), key), -jnp.inf)
        largest = jnp.max(masked, axis=1, keepdims=True)
        raised = jnp.exp2((masked - largest) * RATE)
        totals = jnp.sum(raised, axis=1, keepdims=True)
        mix_ref[g] = jnp.dot(
            raised.astype(jnp.bfloat16), value, preferred_element_type=jnp.float32
        )
        stat_ref[g] = jnp.where(
            lax.broadcasted_iota(jnp.int32, (rows, HD), 1) < 64, largest, totals
        )


def own_attention(queries, pieces):
    rows = GROUP * ROWS
    return pl.pallas_call(
        own_kernel,
        out_shape=(
            jax.ShapeDtypeStruct((KV, rows, HD), jnp.float32),
            jax.ShapeDtypeStruct((KV, rows, HD), jnp.float32),
        ),
        cost_estimate=pl.CostEstimate(
            flops=4 * KV * rows * BLK * HD, bytes_accessed=4 << 20, transcendentals=KV * rows * BLK
        ),
        compiler_params=pltpu.CompilerParams(vmem_limit_bytes=32 << 20),
        name="own_attention",
    )(queries, *pieces)


def anchor_kernel(first, q_ref, mix_ref, stat_ref, a0, a1, a2, a3, b_ref, out_ref):
    blk, hd = lax.axis_index("blk"), lax.axis_index("hd")
    anchored = blk * 2 + (hd >> 2) > 0
    swap = (blk & 1) == 1
    mine = (a0, a1, a2, a3)

    def head(g, key, value):
        scores = jnp.where(anchored, raw_scores(stacked_queries(q_ref, g), key), -jnp.inf)
        old = stat_ref[g][:, 0:1]
        old_totals = stat_ref[g][:, 64:65]
        largest = jnp.maximum(jnp.max(scores, axis=1, keepdims=True), old)
        raised = jnp.exp2((scores - largest) * RATE)
        keep = jnp.exp2((old - largest) * RATE)
        totals = jnp.sum(raised, axis=1, keepdims=True) + old_totals * keep
        mixture = (
            jnp.dot(raised.astype(jnp.bfloat16), value, preferred_element_type=jnp.float32)
            + mix_ref[g] * keep
        )
        result = (mixture / totals).astype(jnp.bfloat16)
        for i in range(GROUP):
            out_ref[:, (g * GROUP + i) * HD : (g * GROUP + i + 1) * HD] = result[
                i * ROWS : (i + 1) * ROWS
            ]

    for g in range(KV):
        column = (g % HALF) * HD
        here = swap == (g >= HALF)
        parts = []
        for offset in (column, column + HALF * HD):
            near = jnp.concatenate([r[:, offset : offset + HD] for r in mine], axis=0)
            parts.append(jnp.where(here, near, b_ref[:, offset : offset + HD]))
        head(g, *parts)


def anchor_attention(queries, mixture, stats, mine, other):
    rows = GROUP * ROWS
    return pl.pallas_call(
        functools.partial(anchor_kernel, True),
        out_shape=jax.ShapeDtypeStruct((ROWS, H * HD), jnp.bfloat16),
        cost_estimate=pl.CostEstimate(
            flops=4 * KV * rows * BLK * HD, bytes_accessed=4 << 20, transcendentals=KV * rows * BLK
        ),
        compiler_params=pltpu.CompilerParams(vmem_limit_bytes=32 << 20),
        name="anchor_attention",
    )(queries, mixture, stats, *mine, other)


def shards(queries, keys, values):
    _, _, _, core = whereabouts()
    width = HALF * HD
    low = jnp.concatenate([keys[:, :width], values[:, :width]], axis=1)
    high = jnp.concatenate([keys[:, width:], values[:, width:]], axis=1)
    both = jnp.concatenate([low, high], axis=1)
    across = lax.ppermute(high, AXES, [(place(0, y, 0, 0), place(0, y, 0, 1)) for y in range(4)])
    pieces = [both] + [along_y(both, step, False) for step in (1, 2, 3)]
    anchor, (mixture, stats) = spread(
        jnp.where(core == 1, across, low), own_attention(queries, pieces)
    )
    mine = [anchor] + [along_y(anchor, step, True) for step in (1, 3, 2)]
    swaps = [(place(x, y, z, c), place(x, y, z, 1 - c)) for x in range(4) for y in range(4) for z in range(8) for c in range(2)]
    other = lax.ppermute(jnp.concatenate(mine, axis=0), AXES, swaps)
    return anchor_attention(queries, mixture, stats, mine, other)


def solution(mesh):
    rows = P(("blk", "hd"), None)
    return jax.shard_map(
        shards, mesh=mesh, in_specs=(rows, rows, rows), out_specs=rows, check_vma=False
    )
```

```python
import functools

import jax
import jax.numpy as jnp
import numpy as np
from jax import lax
from jax.experimental import pallas as pl
from jax.experimental.pallas import tpu as pltpu
from jax.sharding import PartitionSpec as P

H = 32
KV = 8
HD = 128
BLK = 256
ROWS = 64
GROUP = H // KV
HALF = KV // 2
RATE = HD ** (-0.5) * 1.4426950408889634
AXES = ("blk", "hd")


def place(x, y, z, core):
    return (z * 4 + (x % 2) * 2 + core) * 8 + (x // 2) * 4 + y


def whereabouts():
    blk, hd = lax.axis_index("blk"), lax.axis_index("hd")
    return (hd >> 2) * 2 + ((blk >> 1) & 1), hd & 3, blk >> 2, blk & 1


def on_chips(chips):
    x, _, z, _ = whereabouts()
    bits = 0
    for a, b in chips:
        bits |= 1 << (a * 8 + b)
    shift = (x * 8 + z).astype(jnp.uint32)
    return ((jnp.uint32(np.uint32(bits)) >> shift) & 1) == 1


def chips():
    return [(x, y, z) for x in range(4) for y in range(4) for z in range(8)]


def along_y(array, step):
    pairs = [
        (place(x, y, z, core), place(x, (y + step) % 4, z, core))
        for x, y, z in chips()
        for core in range(2)
    ]
    return lax.ppermute(array, AXES, pairs)


def to_other_core(array):
    pairs = [(place(x, y, z, c), place(x, y, z, 1 - c)) for x, y, z in chips() for c in range(2)]
    return lax.ppermute(array, AXES, pairs)


def spread(piece, beside):
    have = [(0, 0)]
    for number, level in enumerate(LEVELS):
        came = []
        for step in level:
            moves = [((x, z), b) for x, z in have for b in step(x, z)]
            pairs = [
                (place(a[0], y, a[1], core), place(b[0], y, b[1], core))
                for a, b in moves
                for y in range(4)
                for core in range(2)
            ]
            came.append((lax.ppermute(piece, AXES, pairs), [b for _, b in moves]))
        if number == 2:
            got, beside = lax.optimization_barrier(([g for g, _ in came], beside))
            came = [(g, to) for g, (_, to) in zip(got, came)]
        for got, to in came:
            piece = jnp.where(on_chips(to), got, piece)
            have = have + to
    return piece, beside


def by(dx, dz):
    return lambda x, z: [((x + dx) % 4, (z + dz) % 8)]


LEVELS = (
    (by(1, 0), by(3, 0), by(2, 0)),
    (by(0, 2), by(0, 6), by(0, 4)),
    (by(0, 1),),
)


def stacked_queries(q_ref, start):
    return jnp.concatenate(
        [q_ref[:, pl.ds(start + i * HD, HD)] for i in range(GROUP)], axis=0
    )


def raw_scores(query, key):
    return lax.dot_general(query, key, (((1,), (1,)), ((), ())), preferred_element_type=jnp.float32)


def own_kernel(q_ref, own_ref, near_ref, far_ref, low_ref, high_ref, state_ref):
    y = lax.axis_index("hd") & 3
    rows = GROUP * ROWS
    row = lax.broadcasted_iota(jnp.int32, (rows, BLK), 0) & (ROWS - 1)
    column = lax.broadcasted_iota(jnp.int32, (rows, BLK), 1)
    behind = jnp.where(y >= 1, 2 * ROWS, 0)
    ahead = jnp.where(y == 3, 3 * ROWS, 0)
    across = jnp.where(y >= 2, 4 * ROWS, 0)
    end = jnp.where(
        column < ROWS,
        row + 1,
        jnp.where(column < 2 * ROWS, behind, jnp.where(column < 3 * ROWS, ahead, across)),
    )
    visible = column < end
    for g in range(KV):
        base = (g // HALF) * 2 * HALF * HD + (g % HALF) * HD
        far = low_ref if g < HALF else high_ref

        def part(base, offset):
            return jnp.concatenate(
                [r[:, base : base + HD] for r in (own_ref, near_ref, far_ref)]
                + [far[:, offset : offset + HD]],
                axis=0,
            )

        key = part(base, (g % HALF) * HD)
        value = part(base + HALF * HD, (HALF + g % HALF) * HD)
        masked = jnp.where(visible, raw_scores(stacked_queries(q_ref, g * GROUP * HD), key), -jnp.inf)
        largest = jnp.max(masked, axis=1, keepdims=True)
        raised = jnp.exp2((masked - largest) * RATE)
        totals = jnp.sum(raised, axis=1, keepdims=True)
        state_ref[g, :, :HD] = jnp.dot(
            raised.astype(jnp.bfloat16), value, preferred_element_type=jnp.float32
        )
        state_ref[g, :, HD : 2 * HD] = jnp.broadcast_to(largest, (rows, HD))
        state_ref[g, :, 2 * HD :] = jnp.broadcast_to(totals, (rows, HD))


def own_attention(queries, pieces):
    rows = GROUP * ROWS
    return pl.pallas_call(
        own_kernel,
        out_shape=jax.ShapeDtypeStruct((KV, rows, 3 * HD), jnp.float32),
        cost_estimate=pl.CostEstimate(
            flops=4 * KV * rows * BLK * HD, bytes_accessed=4 << 20, transcendentals=KV * rows * BLK
        ),
        compiler_params=pltpu.CompilerParams(vmem_limit_bytes=12 << 20),
        name="own_attention",
    )(queries, *pieces)


def anchor_kernel(last, q_ref, state_ref, *refs):
    blk, hd = lax.axis_index("blk"), lax.axis_index("hd")
    anchored = blk * 2 + (hd >> 2) > 0
    half = 1 - (blk & 1) if last else blk & 1
    width = HALF * GROUP * HD
    out_ref = refs[-1]
    pieces = refs[1:-1] if last else refs[:-1]
    for g in range(HALF):
        key = jnp.concatenate([r[:, g * HD : (g + 1) * HD] for r in pieces], axis=0)
        value = jnp.concatenate(
            [r[:, (HALF + g) * HD : (HALF + g + 1) * HD] for r in pieces], axis=0
        )
        head = half * HALF + g
        start = pl.multiple_of(head * GROUP * HD, GROUP * HD)
        scores = raw_scores(stacked_queries(q_ref, start), key)
        scores = jnp.where(anchored, scores, -jnp.inf)
        state = state_ref[head]
        old = state[:, HD : 2 * HD]
        largest = jnp.maximum(jnp.max(scores, axis=1, keepdims=True), old)
        raised = jnp.exp2((scores - jnp.concatenate([largest, largest], axis=1)) * RATE)
        keep = jnp.exp2((old - largest) * RATE)
        totals = jnp.sum(raised, axis=1, keepdims=True) + state[:, 2 * HD :] * keep
        mixture = jnp.dot(raised.astype(jnp.bfloat16), value, preferred_element_type=jnp.float32)
        result = ((mixture + state[:, :HD] * keep) / totals).astype(jnp.bfloat16)
        base = start if last else g * GROUP * HD
        for i in range(GROUP):
            out_ref[:, pl.ds(base + i * HD, HD)] = result[i * ROWS : (i + 1) * ROWS]
    if last:
        out_ref[:, pl.ds(pl.multiple_of((1 - half) * width, width), width)] = refs[0][...]


def anchor_attention(last, queries, own, *arrays):
    rows = GROUP * ROWS
    width = H * HD if last else H * HD // 2
    return pl.pallas_call(
        functools.partial(anchor_kernel, last),
        out_shape=jax.ShapeDtypeStruct((ROWS, width), jnp.bfloat16),
        cost_estimate=pl.CostEstimate(
            flops=4 * HALF * rows * BLK * HD,
            bytes_accessed=2 << 20,
            transcendentals=HALF * rows * BLK,
        ),
        compiler_params=pltpu.CompilerParams(vmem_limit_bytes=12 << 20),
        name="anchor_attention",
    )(queries, own, *arrays)


def shards(queries, keys, values):
    _, _, _, core = whereabouts()
    width = HALF * HD
    low = jnp.concatenate([keys[:, :width], values[:, :width]], axis=1)
    high = jnp.concatenate([keys[:, width:], values[:, width:]], axis=1)
    both = jnp.concatenate([low, high], axis=1)
    behind, ahead = along_y(both, 1), along_y(both, 3)
    pieces = [
        both,
        behind,
        ahead,
        along_y(behind[:, : 2 * width], 1),
        along_y(ahead[:, 2 * width :], 3),
    ]
    own = own_attention(queries, pieces)
    across = to_other_core(high)
    anchor, own = spread(jnp.where(core == 1, across, low), own)
    mine = [anchor] + [along_y(anchor, step) for step in (1, 3, 2)]
    other = to_other_core(jnp.concatenate(mine, axis=0))
    first = anchor_attention(False, queries, own, *mine)
    return anchor_attention(True, queries, own, first, other)


def solution(mesh):
    rows = P(("blk", "hd"), None)
    return jax.shard_map(
        shards, mesh=mesh, in_specs=(rows, rows, rows), out_specs=rows, check_vma=False
    )
```

```python
import functools

import jax
import jax.numpy as jnp
import numpy as np
from jax import lax
from jax.experimental import pallas as pl
from jax.experimental.pallas import tpu as pltpu
from jax.sharding import PartitionSpec as P

H = 32
KV = 8
HD = 128
BLK = 256
ROWS = 64
GROUP = H // KV
HALF = KV // 2
RATE = HD ** (-0.5) * 1.4426950408889634
AXES = ("blk", "hd")


def place(x, y, z, core):
    return (z * 4 + (x % 2) * 2 + core) * 8 + (x // 2) * 4 + y


def whereabouts():
    blk, hd = lax.axis_index("blk"), lax.axis_index("hd")
    return (hd >> 2) * 2 + ((blk >> 1) & 1), hd & 3, blk >> 2, blk & 1


def on_chips(chips):
    x, _, z, _ = whereabouts()
    bits = 0
    for a, b in chips:
        bits |= 1 << (a * 8 + b)
    shift = (x * 8 + z).astype(jnp.uint32)
    return ((jnp.uint32(np.uint32(bits)) >> shift) & 1) == 1


def chips():
    return [(x, y, z) for x in range(4) for y in range(4) for z in range(8)]


def along_y(array, step):
    pairs = [
        (place(x, y, z, core), place(x, (y + step) % 4, z, core))
        for x, y, z in chips()
        for core in range(2)
    ]
    return lax.ppermute(array, AXES, pairs)


def to_other_core(array):
    pairs = [(place(x, y, z, c), place(x, y, z, 1 - c)) for x, y, z in chips() for c in range(2)]
    return lax.ppermute(array, AXES, pairs)


def spread(piece, beside):
    have = [(0, 0)]
    for number, level in enumerate(LEVELS):
        came = []
        for step in level:
            moves = [((x, z), b) for x, z in have for b in step(x, z)]
            pairs = [
                (place(a[0], y, a[1], core), place(b[0], y, b[1], core))
                for a, b in moves
                for y in range(4)
                for core in range(2)
            ]
            came.append((lax.ppermute(piece, AXES, pairs), [b for _, b in moves]))
        if number == 1:
            got, beside = lax.optimization_barrier(([g for g, _ in came], beside))
            came = [(g, to) for g, (_, to) in zip(got, came)]
        for got, to in came:
            piece = jnp.where(on_chips(to), got, piece)
            have = have + to
    return piece, beside


def by(dx, dz):
    return lambda x, z: [((x + dx) % 4, (z + dz) % 8)]


LEVELS = (
    (by(1, 0), by(3, 0), by(2, 0)),
    (by(0, 2), by(0, 6)),
    (lambda x, z: {2: [(x, 4)], 6: [(x, 5)]}.get(z, []), lambda x, z: [(x, {0: 1, 2: 3, 6: 7}[z])]),
)


def stacked_queries(q_ref, start):
    return jnp.concatenate(
        [q_ref[:, pl.ds(start + i * HD, HD)] for i in range(GROUP)], axis=0
    )


def raw_scores(query, key):
    return lax.dot_general(query, key, (((1,), (1,)), ((), ())), preferred_element_type=jnp.float32)


def own_kernel(q_ref, own_ref, near_ref, far_ref, low_ref, high_ref, state_ref):
    y = lax.axis_index("hd") & 3
    rows = GROUP * ROWS
    row = lax.broadcasted_iota(jnp.int32, (rows, BLK), 0) & (ROWS - 1)
    column = lax.broadcasted_iota(jnp.int32, (rows, BLK), 1)
    behind = jnp.where(y >= 1, 2 * ROWS, 0)
    ahead = jnp.where(y == 3, 3 * ROWS, 0)
    across = jnp.where(y >= 2, 4 * ROWS, 0)
    end = jnp.where(
        column < ROWS,
        row + 1,
        jnp.where(column < 2 * ROWS, behind, jnp.where(column < 3 * ROWS, ahead, across)),
    )
    visible = column < end
    for g in range(KV):
        base = (g // HALF) * 2 * HALF * HD + (g % HALF) * HD
        far = low_ref if g < HALF else high_ref

        def part(base, offset):
            return jnp.concatenate(
                [r[:, base : base + HD] for r in (own_ref, near_ref, far_ref)]
                + [far[:, offset : offset + HD]],
                axis=0,
            )

        key = part(base, (g % HALF) * HD)
        value = part(base + HALF * HD, (HALF + g % HALF) * HD)
        masked = jnp.where(visible, raw_scores(stacked_queries(q_ref, g * GROUP * HD), key), -jnp.inf)
        largest = jnp.max(masked, axis=1, keepdims=True)
        raised = jnp.exp2((masked - largest) * RATE)
        totals = jnp.sum(raised, axis=1, keepdims=True)
        state_ref[g, :, :HD] = jnp.dot(
            raised.astype(jnp.bfloat16), value, preferred_element_type=jnp.float32
        )
        state_ref[g, :, HD : 2 * HD] = jnp.broadcast_to(largest, (rows, HD))
        state_ref[g, :, 2 * HD :] = jnp.broadcast_to(totals, (rows, HD))


def own_attention(queries, pieces):
    rows = GROUP * ROWS
    return pl.pallas_call(
        own_kernel,
        out_shape=jax.ShapeDtypeStruct((KV, rows, 3 * HD), jnp.float32),
        cost_estimate=pl.CostEstimate(
            flops=4 * KV * rows * BLK * HD, bytes_accessed=4 << 20, transcendentals=KV * rows * BLK
        ),
        compiler_params=pltpu.CompilerParams(vmem_limit_bytes=12 << 20),
        name="own_attention",
    )(queries, *pieces)


def anchor_kernel(last, q_ref, state_ref, *refs):
    blk, hd = lax.axis_index("blk"), lax.axis_index("hd")
    anchored = blk * 2 + (hd >> 2) > 0
    half = 1 - (blk & 1) if last else blk & 1
    width = HALF * GROUP * HD
    out_ref = refs[-1]
    pieces = refs[1:-1] if last else refs[:-1]
    for g in range(HALF):
        key = jnp.concatenate([r[:, g * HD : (g + 1) * HD] for r in pieces], axis=0)
        value = jnp.concatenate(
            [r[:, (HALF + g) * HD : (HALF + g + 1) * HD] for r in pieces], axis=0
        )
        head = half * HALF + g
        start = pl.multiple_of(head * GROUP * HD, GROUP * HD)
        scores = raw_scores(stacked_queries(q_ref, start), key)
        scores = jnp.where(anchored, scores, -jnp.inf)
        state = state_ref[head]
        old = state[:, HD : 2 * HD]
        largest = jnp.maximum(jnp.max(scores, axis=1, keepdims=True), old)
        raised = jnp.exp2((scores - jnp.concatenate([largest, largest], axis=1)) * RATE)
        keep = jnp.exp2((old - largest) * RATE)
        totals = jnp.sum(raised, axis=1, keepdims=True) + state[:, 2 * HD :] * keep
        mixture = jnp.dot(raised.astype(jnp.bfloat16), value, preferred_element_type=jnp.float32)
        result = ((mixture + state[:, :HD] * keep) / totals).astype(jnp.bfloat16)
        base = start if last else g * GROUP * HD
        for i in range(GROUP):
            out_ref[:, pl.ds(base + i * HD, HD)] = result[i * ROWS : (i + 1) * ROWS]
    if last:
        out_ref[:, pl.ds(pl.multiple_of((1 - half) * width, width), width)] = refs[0][...]


def anchor_attention(last, queries, own, *arrays):
    rows = GROUP * ROWS
    width = H * HD if last else H * HD // 2
    return pl.pallas_call(
        functools.partial(anchor_kernel, last),
        out_shape=jax.ShapeDtypeStruct((ROWS, width), jnp.bfloat16),
        cost_estimate=pl.CostEstimate(
            flops=4 * HALF * rows * BLK * HD,
            bytes_accessed=2 << 20,
            transcendentals=HALF * rows * BLK,
        ),
        compiler_params=pltpu.CompilerParams(vmem_limit_bytes=12 << 20),
        name="anchor_attention",
    )(queries, own, *arrays)


def shards(queries, keys, values):
    _, _, _, core = whereabouts()
    width = HALF * HD
    low = jnp.concatenate([keys[:, :width], values[:, :width]], axis=1)
    high = jnp.concatenate([keys[:, width:], values[:, width:]], axis=1)
    both = jnp.concatenate([low, high], axis=1)
    behind, ahead = along_y(both, 1), along_y(both, 3)
    across = to_other_core(high)
    anchor, (behind, ahead) = spread(jnp.where(core == 1, across, low), (behind, ahead))
    far = along_y(behind[:, : 2 * width], 1), along_y(ahead[:, 2 * width :], 3)
    own = own_attention(queries, [both, behind, ahead, *far])
    mine = [anchor] + [along_y(anchor, step) for step in (2, 1, 3)]
    joined, own = lax.optimization_barrier((jnp.concatenate(mine, axis=0), own))
    other = to_other_core(joined)
    first = anchor_attention(False, queries, own, *mine)
    return anchor_attention(True, queries, own, first, other)


def solution(mesh):
    rows = P(("blk", "hd"), None)
    return jax.shard_map(
        shards, mesh=mesh, in_specs=(rows, rows, rows), out_specs=rows, check_vma=False
    )
```

```python
import functools

import jax
import jax.numpy as jnp
import numpy as np
from jax import lax
from jax.experimental import pallas as pl
from jax.experimental.pallas import tpu as pltpu
from jax.sharding import PartitionSpec as P

H = 32
KV = 8
HD = 128
BLK = 256
ROWS = 64
GROUP = H // KV
HALF = KV // 2
RATE = HD ** (-0.5) * 1.4426950408889634
AXES = ("blk", "hd")


def place(x, y, z, core):
    return (z * 4 + (x % 2) * 2 + core) * 8 + (x // 2) * 4 + y


def whereabouts():
    blk, hd = lax.axis_index("blk"), lax.axis_index("hd")
    return (hd >> 2) * 2 + ((blk >> 1) & 1), hd & 3, blk >> 2, blk & 1


def on_chips(chips):
    x, _, z, _ = whereabouts()
    bits = 0
    for a, b in chips:
        bits |= 1 << (a * 8 + b)
    shift = (x * 8 + z).astype(jnp.uint32)
    return ((jnp.uint32(np.uint32(bits)) >> shift) & 1) == 1


def chips():
    return [(x, y, z) for x in range(4) for y in range(4) for z in range(8)]


def along_y(array, step):
    pairs = [
        (place(x, y, z, core), place(x, (y + step) % 4, z, core))
        for x, y, z in chips()
        for core in range(2)
    ]
    return lax.ppermute(array, AXES, pairs)


def to_other_core(array):
    pairs = [(place(x, y, z, c), place(x, y, z, 1 - c)) for x, y, z in chips() for c in range(2)]
    return lax.ppermute(array, AXES, pairs)


def spread(piece, beside):
    have = [(0, 0)]
    for number, level in enumerate(LEVELS):
        came = []
        for step in level:
            moves = [((x, z), b) for x, z in have for b in step(x, z)]
            pairs = [
                (place(a[0], y, a[1], core), place(b[0], y, b[1], core))
                for a, b in moves
                for y in range(4)
                for core in range(2)
            ]
            came.append((lax.ppermute(piece, AXES, pairs), [b for _, b in moves]))
        if number == 1:
            got, beside = lax.optimization_barrier(([g for g, _ in came], beside))
            came = [(g, to) for g, (_, to) in zip(got, came)]
        for got, to in came:
            piece = jnp.where(on_chips(to), got, piece)
            have = have + to
    return piece, beside


def by(dx, dz):
    return lambda x, z: [((x + dx) % 4, (z + dz) % 8)]


LEVELS = (
    (by(1, 0), by(3, 0), by(2, 0)),
    (by(0, 3), by(0, 6)),
    (
        lambda x, z: [(x, {3: 4, 6: 5}[z])] if z else [],
        lambda x, z: [(x, {0: 1, 3: 2, 6: 7}[z])],
    ),
)


def stacked_queries(q_ref, start):
    return jnp.concatenate(
        [q_ref[:, pl.ds(start + i * HD, HD)] for i in range(GROUP)], axis=0
    )


def raw_scores(query, key):
    return lax.dot_general(query, key, (((1,), (1,)), ((), ())), preferred_element_type=jnp.float32)


def own_kernel(q_ref, own_ref, near_ref, far_ref, low_ref, high_ref, state_ref):
    y = lax.axis_index("hd") & 3
    rows = GROUP * ROWS
    row = lax.broadcasted_iota(jnp.int32, (rows, BLK), 0) & (ROWS - 1)
    column = lax.broadcasted_iota(jnp.int32, (rows, BLK), 1)
    behind = jnp.where(y >= 1, 2 * ROWS, 0)
    ahead = jnp.where(y == 3, 3 * ROWS, 0)
    across = jnp.where(y >= 2, 4 * ROWS, 0)
    end = jnp.where(
        column < ROWS,
        row + 1,
        jnp.where(column < 2 * ROWS, behind, jnp.where(column < 3 * ROWS, ahead, across)),
    )
    visible = column < end
    for g in range(KV):
        base = (g // HALF) * 2 * HALF * HD + (g % HALF) * HD
        far = low_ref if g < HALF else high_ref

        def part(base, offset):
            return jnp.concatenate(
                [r[:, base : base + HD] for r in (own_ref, near_ref, far_ref)]
                + [far[:, offset : offset + HD]],
                axis=0,
            )

        key = part(base, (g % HALF) * HD)
        value = part(base + HALF * HD, (HALF + g % HALF) * HD)
        masked = jnp.where(visible, raw_scores(stacked_queries(q_ref, g * GROUP * HD), key), -jnp.inf)
        largest = jnp.max(masked, axis=1, keepdims=True)
        raised = jnp.exp2((masked - largest) * RATE)
        totals = jnp.sum(raised, axis=1, keepdims=True)
        state_ref[g, :, :HD] = jnp.dot(
            raised.astype(jnp.bfloat16), value, preferred_element_type=jnp.float32
        )
        state_ref[g, :, HD : 2 * HD] = jnp.broadcast_to(largest, (rows, HD))
        state_ref[g, :, 2 * HD :] = jnp.broadcast_to(totals, (rows, HD))


def own_attention(queries, pieces):
    rows = GROUP * ROWS
    return pl.pallas_call(
        own_kernel,
        out_shape=jax.ShapeDtypeStruct((KV, rows, 3 * HD), jnp.float32),
        cost_estimate=pl.CostEstimate(
            flops=4 * KV * rows * BLK * HD, bytes_accessed=4 << 20, transcendentals=KV * rows * BLK
        ),
        compiler_params=pltpu.CompilerParams(vmem_limit_bytes=12 << 20),
        name="own_attention",
    )(queries, *pieces)


def anchor_kernel(last, q_ref, state_ref, *refs):
    blk, hd = lax.axis_index("blk"), lax.axis_index("hd")
    anchored = blk * 2 + (hd >> 2) > 0
    half = 1 - (blk & 1) if last else blk & 1
    width = HALF * GROUP * HD
    out_ref = refs[-1]
    pieces = refs[1:-1] if last else refs[:-1]
    for g in range(HALF):
        key = jnp.concatenate([r[:, g * HD : (g + 1) * HD] for r in pieces], axis=0)
        value = jnp.concatenate(
            [r[:, (HALF + g) * HD : (HALF + g + 1) * HD] for r in pieces], axis=0
        )
        head = half * HALF + g
        start = pl.multiple_of(head * GROUP * HD, GROUP * HD)
        scores = raw_scores(stacked_queries(q_ref, start), key)
        scores = jnp.where(anchored, scores, -jnp.inf)
        state = state_ref[head]
        old = state[:, HD : 2 * HD]
        largest = jnp.maximum(jnp.max(scores, axis=1, keepdims=True), old)
        raised = jnp.exp2((scores - jnp.concatenate([largest, largest], axis=1)) * RATE)
        keep = jnp.exp2((old - largest) * RATE)
        totals = jnp.sum(raised, axis=1, keepdims=True) + state[:, 2 * HD :] * keep
        mixture = jnp.dot(raised.astype(jnp.bfloat16), value, preferred_element_type=jnp.float32)
        result = ((mixture + state[:, :HD] * keep) / totals).astype(jnp.bfloat16)
        base = start if last else g * GROUP * HD
        for i in range(GROUP):
            out_ref[:, pl.ds(base + i * HD, HD)] = result[i * ROWS : (i + 1) * ROWS]
    if last:
        out_ref[:, pl.ds(pl.multiple_of((1 - half) * width, width), width)] = refs[0][...]


def anchor_attention(last, queries, own, *arrays):
    rows = GROUP * ROWS
    width = H * HD if last else H * HD // 2
    return pl.pallas_call(
        functools.partial(anchor_kernel, last),
        out_shape=jax.ShapeDtypeStruct((ROWS, width), jnp.bfloat16),
        cost_estimate=pl.CostEstimate(
            flops=4 * HALF * rows * BLK * HD,
            bytes_accessed=2 << 20,
            transcendentals=HALF * rows * BLK,
        ),
        compiler_params=pltpu.CompilerParams(vmem_limit_bytes=12 << 20),
        name="anchor_attention",
    )(queries, own, *arrays)


def shards(queries, keys, values):
    _, _, _, core = whereabouts()
    width = HALF * HD
    low = jnp.concatenate([keys[:, :width], values[:, :width]], axis=1)
    high = jnp.concatenate([keys[:, width:], values[:, width:]], axis=1)
    both = jnp.concatenate([low, high], axis=1)
    behind, ahead = along_y(both, 1), along_y(both, 3)
    across = lax.ppermute(high, AXES, [(place(0, y, 0, 0), place(0, y, 0, 1)) for y in range(4)])
    anchor, (behind, ahead) = spread(jnp.where(core == 1, across, low), (behind, ahead))
    far = along_y(behind[:, : 2 * width], 1), along_y(ahead[:, 2 * width :], 3)
    own = own_attention(queries, [both, behind, ahead, *far])
    mine = [anchor] + [along_y(anchor, step) for step in (2, 1, 3)]
    joined, own = lax.optimization_barrier((jnp.concatenate(mine, axis=0), own))
    other = to_other_core(joined)
    first = anchor_attention(False, queries, own, *mine)
    return anchor_attention(True, queries, own, first, other)


def solution(mesh):
    rows = P(("blk", "hd"), None)
    return jax.shard_map(
        shards, mesh=mesh, in_specs=(rows, rows, rows), out_specs=rows, check_vma=False
    )
```

```python
import functools

import jax
import jax.numpy as jnp
import numpy as np
from jax import lax
from jax.experimental import pallas as pl
from jax.experimental.pallas import tpu as pltpu
from jax.sharding import PartitionSpec as P

H = 32
KV = 8
HD = 128
BLK = 256
ROWS = 64
GROUP = H // KV
HALF = KV // 2
RATE = HD ** (-0.5) * 1.4426950408889634
AXES = ("blk", "hd")


def place(x, y, z, core):
    return (z * 4 + (x % 2) * 2 + core) * 8 + (x // 2) * 4 + y


def whereabouts():
    blk, hd = lax.axis_index("blk"), lax.axis_index("hd")
    return (hd >> 2) * 2 + ((blk >> 1) & 1), hd & 3, blk >> 2, blk & 1


def on_chips(chips):
    x, _, z, _ = whereabouts()
    bits = 0
    for a, b in chips:
        bits |= 1 << (a * 8 + b)
    shift = (x * 8 + z).astype(jnp.uint32)
    return ((jnp.uint32(np.uint32(bits)) >> shift) & 1) == 1


def chips():
    return [(x, y, z) for x in range(4) for y in range(4) for z in range(8)]


def along_y(array, step):
    pairs = [
        (place(x, y, z, core), place(x, (y + step) % 4, z, core))
        for x, y, z in chips()
        for core in range(2)
    ]
    return lax.ppermute(array, AXES, pairs)


def to_other_core(array):
    pairs = [(place(x, y, z, c), place(x, y, z, 1 - c)) for x, y, z in chips() for c in range(2)]
    return lax.ppermute(array, AXES, pairs)


def spread(piece, beside):
    have = [(0, 0)]
    for number, level in enumerate(LEVELS):
        came = []
        for step in level:
            moves = [((x, z), b) for x, z in have for b in step(x, z)]
            pairs = [
                (place(a[0], y, a[1], core), place(b[0], y, b[1], core))
                for a, b in moves
                for y in range(4)
                for core in range(2)
            ]
            came.append((lax.ppermute(piece, AXES, pairs), [b for _, b in moves]))
        if number == 1:
            got, beside = lax.optimization_barrier(([g for g, _ in came], beside))
            came = [(g, to) for g, (_, to) in zip(got, came)]
        for got, to in came:
            piece = jnp.where(on_chips(to), got, piece)
            have = have + to
    return piece, beside


def by(dx, dz):
    return lambda x, z: [((x + dx) % 4, (z + dz) % 8)]


LEVELS = (
    (by(1, 0), by(3, 0), by(2, 0)),
    (by(0, 3), by(0, 6)),
    (
        lambda x, z: [(x, {3: 4, 6: 5}[z])] if z else [],
        lambda x, z: [(x, {0: 1, 3: 2, 6: 7}[z])],
    ),
)


def stacked_queries(q_ref, start):
    return jnp.concatenate(
        [q_ref[:, pl.ds(start + i * HD, HD)] for i in range(GROUP)], axis=0
    )


def raw_scores(query, key):
    return lax.dot_general(query, key, (((1,), (1,)), ((), ())), preferred_element_type=jnp.float32)


def own_kernel(q_ref, own_ref, near_ref, far_ref, low_ref, high_ref, state_ref):
    y = lax.axis_index("hd") & 3
    rows = GROUP * ROWS
    row = lax.broadcasted_iota(jnp.int32, (rows, BLK), 0) & (ROWS - 1)
    column = lax.broadcasted_iota(jnp.int32, (rows, BLK), 1)
    behind = jnp.where(y >= 1, 2 * ROWS, 0)
    ahead = jnp.where(y == 3, 3 * ROWS, 0)
    across = jnp.where(y >= 2, 4 * ROWS, 0)
    end = jnp.where(
        column < ROWS,
        row + 1,
        jnp.where(column < 2 * ROWS, behind, jnp.where(column < 3 * ROWS, ahead, across)),
    )
    visible = column < end
    for g in range(KV):
        base = (g // HALF) * 2 * HALF * HD + (g % HALF) * HD
        far = low_ref if g < HALF else high_ref

        def part(base, offset):
            return jnp.concatenate(
                [r[:, base : base + HD] for r in (own_ref, near_ref, far_ref)]
                + [far[:, offset : offset + HD]],
                axis=0,
            )

        key = part(base, (g % HALF) * HD)
        value = part(base + HALF * HD, (HALF + g % HALF) * HD)
        masked = jnp.where(visible, raw_scores(stacked_queries(q_ref, g * GROUP * HD), key), -jnp.inf)
        largest = jnp.max(masked, axis=1, keepdims=True)
        raised = jnp.exp2((masked - largest) * RATE)
        totals = jnp.sum(raised, axis=1, keepdims=True)
        state_ref[g, :, :HD] = jnp.dot(
            raised.astype(jnp.bfloat16), value, preferred_element_type=jnp.float32
        )
        state_ref[g, :, HD : 2 * HD] = jnp.broadcast_to(largest, (rows, HD))
        state_ref[g, :, 2 * HD :] = jnp.broadcast_to(totals, (rows, HD))


def own_attention(queries, pieces):
    rows = GROUP * ROWS
    return pl.pallas_call(
        own_kernel,
        out_shape=jax.ShapeDtypeStruct((KV, rows, 3 * HD), jnp.float32),
        cost_estimate=pl.CostEstimate(
            flops=4 * KV * rows * BLK * HD, bytes_accessed=4 << 20, transcendentals=KV * rows * BLK
        ),
        compiler_params=pltpu.CompilerParams(vmem_limit_bytes=12 << 20),
        name="own_attention",
    )(queries, *pieces)


def anchor_kernel(last, q_ref, state_ref, *refs):
    blk, hd = lax.axis_index("blk"), lax.axis_index("hd")
    anchored = blk * 2 + (hd >> 2) > 0
    half = 1 - (blk & 1) if last else blk & 1
    out_ref, held_ref, sems = refs[-3:]
    pieces = refs[1:-3] if last else refs[:-3]
    width = GROUP * HD
    copies = []
    for g in range(HALF):
        key = jnp.concatenate([r[:, g * HD : (g + 1) * HD] for r in pieces], axis=0)
        value = jnp.concatenate(
            [r[:, (HALF + g) * HD : (HALF + g + 1) * HD] for r in pieces], axis=0
        )
        head = half * HALF + g
        start = pl.multiple_of(head * width, width)
        scores = raw_scores(stacked_queries(q_ref, start), key)
        scores = jnp.where(anchored, scores, -jnp.inf)
        state = state_ref[head]
        old = state[:, HD : 2 * HD]
        largest = jnp.maximum(jnp.max(scores, axis=1, keepdims=True), old)
        raised = jnp.exp2((scores - jnp.concatenate([largest, largest], axis=1)) * RATE)
        keep = jnp.exp2((old - largest) * RATE)
        totals = jnp.sum(raised, axis=1, keepdims=True) + state[:, 2 * HD :] * keep
        mixture = jnp.dot(raised.astype(jnp.bfloat16), value, preferred_element_type=jnp.float32)
        result = ((mixture + state[:, :HD] * keep) / totals).astype(jnp.bfloat16)
        for i in range(GROUP):
            held_ref[g, :, i * HD : (i + 1) * HD] = result[i * ROWS : (i + 1) * ROWS]
        copy = pltpu.make_async_copy(held_ref.at[g], out_ref.at[:, pl.ds(start, width)], sems.at[g])
        copy.start()
        copies.append(copy)
    for copy in copies:
        copy.wait()


def anchor_attention(last, queries, own, *arrays):
    rows = GROUP * ROWS
    near = pl.BlockSpec(memory_space=pltpu.VMEM)
    far = pl.BlockSpec(memory_space=pl.ANY)
    return pl.pallas_call(
        functools.partial(anchor_kernel, last),
        out_shape=jax.ShapeDtypeStruct((ROWS, H * HD), jnp.bfloat16),
        in_specs=[near, near] + [far if last and i == 0 else near for i in range(len(arrays))],
        out_specs=far,
        input_output_aliases={2: 0} if last else {},
        scratch_shapes=[
            pltpu.VMEM((HALF, ROWS, GROUP * HD), jnp.bfloat16),
            pltpu.SemaphoreType.DMA((HALF,)),
        ],
        cost_estimate=pl.CostEstimate(
            flops=4 * HALF * rows * BLK * HD,
            bytes_accessed=2 << 20,
            transcendentals=HALF * rows * BLK,
        ),
        compiler_params=pltpu.CompilerParams(vmem_limit_bytes=12 << 20),
        name="anchor_attention",
    )(queries, own, *arrays)


def shards(queries, keys, values):
    _, _, _, core = whereabouts()
    width = HALF * HD
    low = jnp.concatenate([keys[:, :width], values[:, :width]], axis=1)
    high = jnp.concatenate([keys[:, width:], values[:, width:]], axis=1)
    both = jnp.concatenate([low, high], axis=1)
    behind, ahead = along_y(both, 1), along_y(both, 3)
    across = lax.ppermute(high, AXES, [(place(0, y, 0, 0), place(0, y, 0, 1)) for y in range(4)])
    anchor, (behind, ahead) = spread(jnp.where(core == 1, across, low), (behind, ahead))
    far = along_y(behind[:, : 2 * width], 1), along_y(ahead[:, 2 * width :], 3)
    own = own_attention(queries, [both, behind, ahead, *far])
    mine = [anchor] + [along_y(anchor, step) for step in (2, 1, 3)]
    joined, own = lax.optimization_barrier((jnp.concatenate(mine, axis=0), own))
    other = to_other_core(joined)
    first = anchor_attention(False, queries, own, *mine)
    return anchor_attention(True, queries, own, first, other)


def solution(mesh):
    rows = P(("blk", "hd"), None)
    return jax.shard_map(
        shards, mesh=mesh, in_specs=(rows, rows, rows), out_specs=rows, check_vma=False
    )
```

```python
import functools

import jax
import jax.numpy as jnp
import numpy as np
from jax import lax
from jax.experimental import pallas as pl
from jax.experimental.pallas import tpu as pltpu
from jax.sharding import PartitionSpec as P

H = 32
KV = 8
HD = 128
BLK = 256
ROWS = 64
GROUP = H // KV
HALF = KV // 2
RATE = HD ** (-0.5) * 1.4426950408889634
AXES = ("blk", "hd")


def place(x, y, z, core):
    return (z * 4 + (x % 2) * 2 + core) * 8 + (x // 2) * 4 + y


def whereabouts():
    blk, hd = lax.axis_index("blk"), lax.axis_index("hd")
    return (hd >> 2) * 2 + ((blk >> 1) & 1), hd & 3, blk >> 2, blk & 1


def on_chips(chips):
    x, _, z, _ = whereabouts()
    bits = 0
    for a, b in chips:
        bits |= 1 << (a * 8 + b)
    shift = (x * 8 + z).astype(jnp.uint32)
    return ((jnp.uint32(np.uint32(bits)) >> shift) & 1) == 1


def chips():
    return [(x, y, z) for x in range(4) for y in range(4) for z in range(8)]


def along_y(array, step):
    pairs = [
        (place(x, y, z, core), place(x, (y + step) % 4, z, core))
        for x, y, z in chips()
        for core in range(2)
    ]
    return lax.ppermute(array, AXES, pairs)


def to_other_core(array):
    pairs = [(place(x, y, z, c), place(x, y, z, 1 - c)) for x, y, z in chips() for c in range(2)]
    return lax.ppermute(array, AXES, pairs)


def spread(piece, beside):
    have = [(0, 0)]
    for number, level in enumerate(LEVELS):
        came = []
        for step in level:
            moves = [((x, z), b) for x, z in have for b in step(x, z)]
            pairs = [
                (place(a[0], y, a[1], core), place(b[0], y, b[1], core))
                for a, b in moves
                for y in range(4)
                for core in range(2)
            ]
            came.append((lax.ppermute(piece, AXES, pairs), [b for _, b in moves]))
        if number == 1:
            got, beside = lax.optimization_barrier(([g for g, _ in came], beside))
            came = [(g, to) for g, (_, to) in zip(got, came)]
        for got, to in came:
            piece = jnp.where(on_chips(to), got, piece)
            have = have + to
    return piece, beside


def by(dx, dz):
    return lambda x, z: [((x + dx) % 4, (z + dz) % 8)]


LEVELS = (
    (by(1, 0), by(3, 0), by(2, 0)),
    (by(0, 3), by(0, 6)),
    (
        lambda x, z: [(x, {0: 1, 3: 4, 6: 7}[z])] if z in {0: 1, 3: 4, 6: 7} else [],
        lambda x, z: [(x, {3: 2, 6: 5}[z])] if z in {3: 2, 6: 5} else [],
    ),
)


def stacked_queries(q_ref, start):
    return jnp.concatenate(
        [q_ref[:, pl.ds(start + i * HD, HD)] for i in range(GROUP)], axis=0
    )


def raw_scores(query, key):
    return lax.dot_general(query, key, (((1,), (1,)), ((), ())), preferred_element_type=jnp.float32)


def own_kernel(q_ref, own_ref, near_ref, far_ref, low_ref, high_ref, state_ref):
    y = lax.axis_index("hd") & 3
    rows = GROUP * ROWS
    row = lax.broadcasted_iota(jnp.int32, (rows, BLK), 0) & (ROWS - 1)
    column = lax.broadcasted_iota(jnp.int32, (rows, BLK), 1)
    behind = jnp.where(y >= 1, 2 * ROWS, 0)
    ahead = jnp.where(y == 3, 3 * ROWS, 0)
    across = jnp.where(y >= 2, 4 * ROWS, 0)
    end = jnp.where(
        column < ROWS,
        row + 1,
        jnp.where(column < 2 * ROWS, behind, jnp.where(column < 3 * ROWS, ahead, across)),
    )
    visible = column < end
    for g in range(KV):
        base = (g // HALF) * 2 * HALF * HD + (g % HALF) * HD
        far = low_ref if g < HALF else high_ref

        def part(base, offset):
            return jnp.concatenate(
                [r[:, base : base + HD] for r in (own_ref, near_ref, far_ref)]
                + [far[:, offset : offset + HD]],
                axis=0,
            )

        key = part(base, (g % HALF) * HD)
        value = part(base + HALF * HD, (HALF + g % HALF) * HD)
        masked = jnp.where(visible, raw_scores(stacked_queries(q_ref, g * GROUP * HD), key), -jnp.inf)
        largest = jnp.max(masked, axis=1, keepdims=True)
        raised = jnp.exp2((masked - largest) * RATE)
        totals = jnp.sum(raised, axis=1, keepdims=True)
        state_ref[g, :, :HD] = jnp.dot(
            raised.astype(jnp.bfloat16), value, preferred_element_type=jnp.float32
        )
        state_ref[g, :, HD : 2 * HD] = jnp.broadcast_to(largest, (rows, HD))
        state_ref[g, :, 2 * HD :] = jnp.broadcast_to(totals, (rows, HD))


def own_attention(queries, pieces):
    rows = GROUP * ROWS
    return pl.pallas_call(
        own_kernel,
        out_shape=jax.ShapeDtypeStruct((KV, rows, 3 * HD), jnp.float32),
        cost_estimate=pl.CostEstimate(
            flops=4 * KV * rows * BLK * HD, bytes_accessed=4 << 20, transcendentals=KV * rows * BLK
        ),
        compiler_params=pltpu.CompilerParams(vmem_limit_bytes=12 << 20),
        name="own_attention",
    )(queries, *pieces)


def anchor_kernel(last, q_ref, state_ref, *refs):
    blk, hd = lax.axis_index("blk"), lax.axis_index("hd")
    anchored = blk * 2 + (hd >> 2) > 0
    half = 1 - (blk & 1) if last else blk & 1
    out_ref, held_ref, sems = refs[-3:]
    pieces = refs[1:-3] if last else refs[:-3]
    width = GROUP * HD
    copies = []
    for g in range(HALF):
        key = jnp.concatenate([r[:, g * HD : (g + 1) * HD] for r in pieces], axis=0)
        value = jnp.concatenate(
            [r[:, (HALF + g) * HD : (HALF + g + 1) * HD] for r in pieces], axis=0
        )
        head = half * HALF + g
        start = pl.multiple_of(head * width, width)
        scores = raw_scores(stacked_queries(q_ref, start), key)
        scores = jnp.where(anchored, scores, -jnp.inf)
        state = state_ref[head]
        old = state[:, HD : 2 * HD]
        largest = jnp.maximum(jnp.max(scores, axis=1, keepdims=True), old)
        raised = jnp.exp2((scores - jnp.concatenate([largest, largest], axis=1)) * RATE)
        keep = jnp.exp2((old - largest) * RATE)
        totals = jnp.sum(raised, axis=1, keepdims=True) + state[:, 2 * HD :] * keep
        mixture = jnp.dot(raised.astype(jnp.bfloat16), value, preferred_element_type=jnp.float32)
        result = ((mixture + state[:, :HD] * keep) / totals).astype(jnp.bfloat16)
        for i in range(GROUP):
            held_ref[g, :, i * HD : (i + 1) * HD] = result[i * ROWS : (i + 1) * ROWS]
        copy = pltpu.make_async_copy(held_ref.at[g], out_ref.at[:, pl.ds(start, width)], sems.at[g])
        copy.start()
        copies.append(copy)
    for copy in copies:
        copy.wait()


def anchor_attention(last, queries, own, *arrays):
    rows = GROUP * ROWS
    near = pl.BlockSpec(memory_space=pltpu.VMEM)
    far = pl.BlockSpec(memory_space=pl.ANY)
    return pl.pallas_call(
        functools.partial(anchor_kernel, last),
        out_shape=jax.ShapeDtypeStruct((ROWS, H * HD), jnp.bfloat16),
        in_specs=[near, near] + [far if last and i == 0 else near for i in range(len(arrays))],
        out_specs=far,
        input_output_aliases={2: 0} if last else {},
        scratch_shapes=[
            pltpu.VMEM((HALF, ROWS, GROUP * HD), jnp.bfloat16),
            pltpu.SemaphoreType.DMA((HALF,)),
        ],
        cost_estimate=pl.CostEstimate(
            flops=4 * HALF * rows * BLK * HD,
            bytes_accessed=2 << 20,
            transcendentals=HALF * rows * BLK,
        ),
        compiler_params=pltpu.CompilerParams(vmem_limit_bytes=12 << 20),
        name="anchor_attention",
    )(queries, own, *arrays)


def shards(queries, keys, values):
    _, _, _, core = whereabouts()
    width = HALF * HD
    low = jnp.concatenate([keys[:, :width], values[:, :width]], axis=1)
    high = jnp.concatenate([keys[:, width:], values[:, width:]], axis=1)
    both = jnp.concatenate([low, high], axis=1)
    behind, ahead = along_y(both, 1), along_y(both, 3)
    across = lax.ppermute(high, AXES, [(place(0, y, 0, 0), place(0, y, 0, 1)) for y in range(4)])
    anchor, (behind, ahead) = spread(jnp.where(core == 1, across, low), (behind, ahead))
    far = along_y(behind[:, : 2 * width], 1), along_y(ahead[:, 2 * width :], 3)
    own = own_attention(queries, [both, behind, ahead, *far])
    mine = [anchor] + [along_y(anchor, step) for step in (2, 1, 3)]
    joined, own = lax.optimization_barrier((jnp.concatenate(mine, axis=0), own))
    other = to_other_core(joined)
    first = anchor_attention(False, queries, own, *mine)
    return anchor_attention(True, queries, own, first, other)


def solution(mesh):
    rows = P(("blk", "hd"), None)
    return jax.shard_map(
        shards, mesh=mesh, in_specs=(rows, rows, rows), out_specs=rows, check_vma=False
    )
```
